32 devices in a mesh: row: 4 (over y, core), col: 4 (over z), depth: 2 (over x).
Axes of the slice: x: 2, y: 2, z: 4, core: 2. Of those that a mesh axis runs over, the one named last changes fastest.
Arguments:
- x_blocks: bfloat16 [64, 8, 128, 128], P(('row', 'col'), 'depth'), may hold values from -2 to 2
- col_slot: int32 [64, 8], P(('row', 'col'), 'depth'), may hold values from 0 to 3
- out_pos: int32 [4, 4, 192, 2], P('row', 'col'), may hold values from 0 to 15, as said below
- out_count: int32 [4, 4], P('row', 'col'), may hold values from 48 to 192, as said below
Outputs:
- product_blocks: bfloat16 [4, 4, 192, 128, 128], P('row', 'col', 'depth')
The draws below stay inside these ranges and needn't reach their ends.
Inputs may be any that keep to these rules, and one draw needn't show every extreme that they name: `out_pos`: within a tile the listed positions are distinct, local rows below 16 and local columns below 16. Some tile uses all 192 slots; only the first out_count slots of a tile are in use.
All inputs are finite; a program needn't handle non-finite values.
Results may differ from the reference program's by a relative error of at most 0.0048.
Values may be sent and summed in bfloat16 or wider, within the bound.
No kernel may reach another device: no remote copies, remote signals or barrier semaphores. Data moves between devices by JAX's collectives and lax.ppermute only.
A program may use at most 128 MiB of HBM per device.

```python
import jax
import jax.numpy as jnp
from jax import lax

BLOCK = 128
PR = 4
GD = 4
SPREAD = 4
OUT_CAP = 192
TILES_R = 4
TILES_C = 4
NB = 64
NG = 8
TROWS = 16
TCOLS = 16
N_ROW = 4
N_COL = 4
N_DEPTH = 2


def draw_out_pos(key, part):
    key = jax.random.fold_in(key, 11)
    tile_keys = jax.random.split(key, TILES_R * TILES_C)

    def one_tile(tile_key):
        picked = jax.random.permutation(tile_key, TROWS * TCOLS)[:OUT_CAP]
        return jnp.stack([picked // TCOLS, picked % TCOLS], -1).astype(jnp.int32)
    return jax.vmap(one_tile)(tile_keys).reshape(TILES_R, TILES_C, OUT_CAP, 2)


def draw_out_count(key, part):
    key = jax.random.fold_in(key, 12)
    first_key, second_key = jax.random.split(key)
    counts = jax.random.randint(first_key, (TILES_R * TILES_C,), OUT_CAP // 4, OUT_CAP + 1)
    fullest = jax.random.randint(second_key, (), 0, TILES_R * TILES_C)
    counts = counts.at[fullest].set(OUT_CAP)
    return counts.reshape(TILES_R, TILES_C).astype(jnp.int32)


def plant(values, key, low, top_value):
    longest = values.shape.index(max(values.shape))
    spots = []
    for shift in (0, 1):
        where = [jax.random.randint(jax.random.fold_in(key, axis), (), 0, length) for axis, length in enumerate(values.shape)]
        where[longest] = (where[longest] + shift) % values.shape[longest]
        spots.append(tuple(where))
    return values.at[spots[0]].set(low).at[spots[1]].set(top_value)


def levels(stream_key, shape, cuts, least, high):
    level = 1.0
    for axis_at, parts in cuts:
        draws = jax.random.uniform(jax.random.fold_in(jax.random.fold_in(stream_key, 6), axis_at), (parts,), jnp.float32, least / len(cuts), high / len(cuts))
        level = level * jnp.repeat(jnp.exp(draws), shape[axis_at] // parts).reshape((-1,) + (1,) * (len(shape) - 1 - axis_at))
    return level


def normal_values(own_key, shape, width, limit, cuts=(), kind=jnp.bfloat16):
    factor_of = levels(own_key, shape, cuts, -0.22, 0.18) if cuts else 1.0
    values = jax.random.normal(own_key, shape, jnp.float32) * width * factor_of
    return jnp.minimum(jnp.maximum(values, -limit), limit).astype(kind)


def setup_inputs(seed: int = 0) -> dict:
    key_list = jax.random.split(jax.random.key(seed), 5)
    return {
        "x_blocks": normal_values(key_list[0], (NB, NG, BLOCK, BLOCK), 0.3, 2.0, ((0, 16), (1, 2))),
        "col_slot": plant(jax.random.randint(key_list[1], (NB, NG), 0, SPREAD), jax.random.fold_in(key_list[1], 1), 0, SPREAD - 1).astype(jnp.int32),
        "out_pos": draw_out_pos(jax.random.fold_in(key_list[4], 71), 0),
        "out_count": draw_out_count(jax.random.fold_in(key_list[4], 71), 0),
    }


def tile_product(x_blocks, col_slot, rows_here, cols_here, live_here):
    total = jnp.zeros((rows_here.shape[0], BLOCK, BLOCK), jnp.float32)
    for depth_idx in range(N_DEPTH):
        summed = jnp.zeros((rows_here.shape[0], BLOCK, BLOCK), jnp.float32)
        for group_at in range(depth_idx * GD, (depth_idx + 1) * GD):
            left_block = x_blocks[rows_here, group_at].astype(jnp.float32)
            right_block = x_blocks[cols_here, group_at].astype(jnp.float32)
            same_slot = (col_slot[rows_here, group_at] == col_slot[cols_here, group_at]).astype(jnp.float32)
            product = jnp.einsum("sab,scb->sac", left_block, right_block)
            summed = summed + product * same_slot[:, None, None]
        rounded = lax.optimization_barrier(summed.astype(jnp.bfloat16))
        total = total + rounded.astype(jnp.float32)
    return (total * live_here[:, None, None]).astype(jnp.bfloat16)


def reference(x_blocks, col_slot, out_pos, out_count):
    ratio = N_COL // N_ROW
    local_row = out_pos[..., 0]
    local_col = out_pos[..., 1]
    tile_row = jnp.arange(N_ROW, dtype=jnp.int32)[:, None, None]
    tile_col = jnp.arange(N_COL, dtype=jnp.int32)[None, :, None]
    span = N_ROW * PR
    rows_all = (((local_row % span) // PR) * N_COL + tile_row * ratio + local_row // span) * PR + local_row % PR
    cols_all = ((local_col // PR) * N_COL + tile_col) * PR + local_col % PR
    slot_ids = jnp.arange(OUT_CAP, dtype=jnp.int32)[None, None, :]
    live_all = (slot_ids < out_count[:, :, None]).astype(jnp.float32)
    rows_all = rows_all.reshape(N_ROW * N_COL, OUT_CAP).astype(jnp.int32)
    cols_all = cols_all.reshape(N_ROW * N_COL, OUT_CAP).astype(jnp.int32)
    live_all = live_all.reshape(N_ROW * N_COL, OUT_CAP)

    def one_tile(packed):
        return tile_product(x_blocks, col_slot, packed[0], packed[1], packed[2])

    tiles = lax.map(one_tile, (rows_all, cols_all, live_all))
    return tiles.reshape(N_ROW, N_COL, OUT_CAP, BLOCK, BLOCK)
```

```python
import functools

import jax
import jax.numpy as jnp
from jax import lax
from jax.experimental import pallas as pl
from jax.experimental.pallas import tpu as pltpu
from jax.sharding import PartitionSpec as P

KEY_ROWS = 16
SLOTS = 16


def product_kernel(
    n_row, n_depth, n_rows, share, first, last, info, pos, *refs
):
    n = n_row * n_depth
    left_in, right_in = refs[:n], refs[n : 2 * n]
    refs = refs[2 * n :]
    if first:
        total_in = None
    else:
        total_in, refs = refs[0], refs[1:]
    out, left, right, left_keys, right_keys, sems = refs
    block = left.shape[-1]
    count, row, depth = info[0], info[1], info[2]

    @pl.when(pl.program_id(0) == 0)
    def _():
        copies = []
        for e in range(n_depth):
            for t in range(n_row):
                at = e * n_row + t
                for side, (src, dst) in enumerate(((left_in, left), (right_in, right))):
                    copies.append(
                        pltpu.make_async_copy(
                            src[at], dst.at[e, row ^ t], sems.at[side * n + at]
                        )
                    )
        for copy in copies:
            copy.start()
        for copy in copies:
            copy.wait()
        for e in range(n_depth):
            for t in range(n_row):
                for src, dst in ((left, left_keys), (right, right_keys)):
                    dst[e, t] = src[e, t, n_rows * block :, :].astype(jnp.float32)

    for i in range(SLOTS):
        slot = depth * share + pl.program_id(0) * SLOTS + i
        u, v = pos[2 * slot], pos[2 * slot + 1]
        u_at, u_in = lax.div(u, n_rows), lax.rem(u, n_rows)
        v_at, v_in = lax.div(v, n_rows), lax.rem(v, n_rows)
        u_rows = pl.ds(pl.multiple_of(u_in * block, block), block)
        v_rows = pl.ds(pl.multiple_of(v_in * block, block), block)
        lefts, rights = [], []
        for e in range(n_depth):
            same = left_keys[e, u_at, pl.ds(u_in, 1), :] == right_keys[e, v_at, pl.ds(v_in, 1), :]
            same = same.astype(jnp.float32).astype(jnp.bfloat16)
            lefts.append(left[e, u_at, u_rows, :])
            rights.append(right[e, v_at, v_rows, :] * same)
        total = lax.dot_general(
            jnp.concatenate(lefts, 1),
            jnp.concatenate(rights, 1),
            (((1,), (1,)), ((), ())),
            preferred_element_type=jnp.float32,
        )
        if total_in is not None:
            total = total + total_in[i]
        if last:
            total = jnp.where(slot < count, total, 0.0)
        out[i] = total.astype(out.dtype)


def add_products(sizes, n_rows, share, first, last, info, pos, left, right, total):
    n_row, n_depth = sizes
    n = n_row * n_depth
    rows, block = left[0].shape
    slots = pl.BlockSpec((SLOTS, block, block), lambda i: (i, 0, 0))
    in_specs = [pl.BlockSpec(memory_space=pltpu.SMEM)] * 2 + [pl.BlockSpec(memory_space=pl.ANY)] * (2 * n)
    args = [info, pos, *left, *right]
    if not first:
        in_specs.append(slots)
        args.append(total)
    return pl.pallas_call(
        functools.partial(product_kernel, n_row, n_depth, n_rows, share, first, last),
        grid=(share // SLOTS,),
        in_specs=in_specs,
        out_specs=slots,
        out_shape=jax.ShapeDtypeStruct((share, block, block), jnp.bfloat16 if last else jnp.float32),
        scratch_shapes=[
            pltpu.VMEM((n_depth, n_row, rows, block), jnp.bfloat16),
            pltpu.VMEM((n_depth, n_row, rows, block), jnp.bfloat16),
            pltpu.VMEM((n_depth, n_row, KEY_ROWS, block), jnp.float32),
            pltpu.VMEM((n_depth, n_row, KEY_ROWS, block), jnp.float32),
            pltpu.SemaphoreType.DMA((2 * n,)),
        ],
        compiler_params=pltpu.CompilerParams(vmem_limit_bytes=40 * 1024 * 1024),
        cost_estimate=pl.CostEstimate(
            flops=2 * share * n_depth * block**3,
            bytes_accessed=2 * n * rows * block * 2 + share * block * block * 8,
            transcendentals=0,
        ),
    )(*args)


def body(sizes, x_blocks, col_slot, out_pos, out_count):
    n_row, n_col, n_depth = sizes
    n_rows, n_groups, block, _ = x_blocks.shape
    capacity = out_pos.shape[2]
    share = capacity // n_depth
    row, col, depth = lax.axis_index("row"), lax.axis_index("col"), lax.axis_index("depth")
    info = jnp.stack([out_count[0, 0], row, depth]).astype(jnp.int32)
    pos = out_pos[0, 0].reshape(-1)

    def swap_row(value, t):
        return lax.ppermute(value, "row", [(i, i ^ t) for i in range(n_row)])

    def from_depth(value, e):
        return lax.ppermute(value, "depth", [((i + e) % n_depth, i) for i in range(n_depth)])

    def from_both(value, t, e):
        pairs = [
            ((i ^ t) * n_depth + (j + e) % n_depth, i * n_depth + j)
            for i in range(n_row)
            for j in range(n_depth)
        ]
        return lax.ppermute(value, ("row", "depth"), pairs)

    total = None
    for g in range(n_groups):
        keys = jnp.pad(col_slot[:, g].astype(jnp.bfloat16), (0, KEY_ROWS - n_rows))
        own = jnp.concatenate(
            [
                x_blocks[:, g].reshape(n_rows * block, block),
                jnp.broadcast_to(keys[:, None], (KEY_ROWS, block)),
            ]
        )
        right = {(0, 0): own}
        for t in range(0, n_row, 2):
            if t:
                right[t, 0] = swap_row(own, t)
        for e in range(1, n_depth):
            right[0, e] = from_depth(own, e)
        for e in range(1, n_depth):
            for t in range(2, n_row, 2):
                right[t, e] = from_depth(right[t, 0], e) if g % 2 else swap_row(right[0, e], t)
        for t in range(1, n_row, 2):
            for e in range(n_depth):
                right[t, e] = swap_row(right[t - 1, e], 1)
        up, down = [own], [own]
        for k in range(1, n_col):
            up.append(lax.ppermute(up[-1], "col", [(i, i + 1) for i in range(k - 1, n_col - 1)]))
            down.append(lax.ppermute(down[-1], "col", [(i + 1, i) for i in range(n_col - k)]))
        left = {}
        for t in range(n_row):
            far = col - (row ^ t)
            value = own
            for k in range(1, n_col):
                value = jnp.where(far == k, up[k], value)
                value = jnp.where(far == -k, down[k], value)
            left[t, 0] = swap_row(value, t) if t else value
            for e in range(1, n_depth):
                if t >= 2 and (t + g) % 2:
                    left[t, e] = from_both(value, t, e)
                else:
                    left[t, e] = from_depth(left[t, 0], e)
        order = [(t, e) for e in range(n_depth) for t in range(n_row)]
        total = add_products(
            (n_row, n_depth),
            n_rows,
            share,
            g == 0,
            g == n_groups - 1,
            info,
            pos,
            [left[at] for at in order],
            [right[at] for at in order],
            total,
        )
    return total[None, None]


def solution(mesh):
    sizes = tuple(mesh.shape[axis] for axis in ("row", "col", "depth"))
    in_specs = (
        P(("row", "col"), "depth", None, None),
        P(("row", "col"), "depth"),
        P("row", "col", None, None),
        P("row", "col"),
    )
    out_specs = P("row", "col", "depth", None, None)
    return jax.shard_map(
        functools.partial(body, sizes), mesh=mesh, in_specs=in_specs, out_specs=out_specs, check_vma=False
    )
```

```python
import functools

import jax
import jax.numpy as jnp
from jax import lax
from jax.experimental import pallas as pl
from jax.experimental.pallas import tpu as pltpu
from jax.sharding import PartitionSpec as P

SLOTS = 48
KEY_ROWS = 16


def product_kernel(plan, places, info, pos, *refs):
    n_row, n_depth, n_rows, share, slots, n_chunks, per = plan
    given, out, refs = refs[: len(places)], refs[len(places)], refs[len(places) + 1 :]
    panels, tails, keys, sums, sems, tail_sems = refs
    block = out.shape[-1]
    size = per * n_rows * block
    n_keys = tails.shape[3]
    count, row, depth, kind = info[0], info[1], info[2], info[3]
    chunk, step = pl.program_id(0), pl.program_id(1)

    def start(side, c, src, place):
        d, r = lax.rem(depth + place[1], n_depth), row ^ place[0]
        rows = src.at[pl.ds(c * size, size)]
        pltpu.make_async_copy(rows, panels.at[side, c, d, r], sems.at[side, c]).start()
        if c == 0:
            rows = src.at[pl.ds(n_chunks * size, n_keys)]
            pltpu.make_async_copy(rows, tails.at[side, d, r], tail_sems.at[side]).start()

    @pl.when((chunk == 0) & (step == 0))
    def _():
        for c in range(n_chunks):
            for side, which in ((1, 0), (0, 0), (0, 1), (0, 2)):

                @pl.when((kind == which) | (side == 1))
                def _():
                    for src, (place, use) in zip(given, places):
                        if use == which:
                            start(side, c, src, place)

    for c in range(n_chunks):

        @pl.when((chunk == c) & (step == 0))
        def _(c=c):
            for side in (0, 1):
                pltpu.make_async_copy(panels.at[side, c], panels.at[side, c], sems.at[side, c]).wait()
                if c == 0:
                    pltpu.make_async_copy(tails.at[side], tails.at[side], tail_sems.at[side]).wait()
                    for d in range(n_depth):
                        for r in range(n_row):
                            rows = tails[side, d, r].astype(jnp.float32)
                            for g in range(n_chunks * per):
                                for i in range(n_rows):
                                    at = g * n_rows + i
                                    keys[side, r * n_rows + i, pl.ds(g * n_depth + d, 1), :] = rows[at : at + 1]

        @pl.when(chunk == c)
        def _(c=c):
            for k in range(slots):
                slot = step * slots + k
                u, v, u_row, v_row = [pos[4 * slot + i] for i in range(4)]
                same = (keys[0, u] == keys[1, v]).astype(jnp.float32).astype(jnp.bfloat16)
                lefts, rights = [], []
                for g in range(per):
                    for d in range(n_depth):
                        at = g * n_rows * block
                        key = (c * per + g) * n_depth + d
                        lefts.append(block_of(panels, 0, c, d, u_row + at))
                        rights.append(block_of(panels, 1, c, d, v_row + at) * same[key : key + 1])
                total = lax.dot_general(
                    jnp.concatenate(lefts, 1),
                    jnp.concatenate(rights, 1),
                    (((1,), (1,)), ((), ())),
                    preferred_element_type=jnp.float32,
                )
                if c:
                    total = total + sums[slot]
                if c < n_chunks - 1:
                    sums[slot] = total
                else:
                    out[k] = jnp.where(depth * share + slot < count, total, 0.0).astype(out.dtype)


def block_of(panels, side, c, d, start):
    n_row, size, block = panels.shape[3:]
    flat = panels.reshape(*panels.shape[:3], n_row * size, block)
    return flat[side, c, d, pl.ds(pl.multiple_of(start, block), block), :]


def products(plan, info, pos, pieces):
    n_row, n_depth, n_rows, share, slots, n_chunks, per = plan
    block = pieces[0][0].shape[-1]
    size = per * n_rows * block
    n_keys = -(-n_chunks * per * n_rows // KEY_ROWS) * KEY_ROWS
    places = [(place, use) for _, place, use in pieces]
    args = [pltpu.with_memory_space_constraint(value, pltpu.HBM) for value, _, _ in pieces]
    panel_bytes = 2 * n_chunks * n_depth * n_row * size * block * 2
    held = panel_bytes + 2 * slots * block * block * 2 + share * block * block * 4
    return pl.pallas_call(
        functools.partial(product_kernel, plan, places),
        grid=(n_chunks, share // slots),
        in_specs=[pl.BlockSpec(memory_space=pltpu.SMEM)] * 2 + [pl.BlockSpec(memory_space=pl.ANY)] * len(args),
        out_specs=pl.BlockSpec((slots, block, block), lambda c, i: (jnp.where(c == n_chunks - 1, i, 0), 0, 0)),
        out_shape=jax.ShapeDtypeStruct((share, block, block), jnp.bfloat16),
        scratch_shapes=[
            pltpu.VMEM((2, n_chunks, n_depth, n_row, size, block), jnp.bfloat16),
            pltpu.VMEM((2, n_depth, n_row, n_keys, block), jnp.bfloat16),
            pltpu.VMEM((2, n_row * n_rows, -(-n_chunks * per * n_depth // 8) * 8, block), jnp.float32),
            pltpu.VMEM((share, block, block), jnp.float32),
            pltpu.SemaphoreType.DMA((2, n_chunks)),
            pltpu.SemaphoreType.DMA((2,)),
        ],
        compiler_params=pltpu.CompilerParams(vmem_limit_bytes=held + 4 * 1024 * 1024),
        cost_estimate=pl.CostEstimate(
            flops=2 * share * n_depth * n_chunks * per * block**3,
            bytes_accessed=panel_bytes + share * block * block * 2,
            transcendentals=0,
        ),
    )(info, pos, *args)


def after(value, *others):
    return lax.optimization_barrier((value, *others))[0]


def payload(x_blocks, col_slot):
    n_rows, n_groups, block, _ = x_blocks.shape
    n = n_rows * n_groups
    rows = jnp.swapaxes(x_blocks, 0, 1).reshape(n * block, block)
    keys = jnp.pad(jnp.swapaxes(col_slot, 0, 1).reshape(n).astype(x_blocks.dtype), (0, -n % KEY_ROWS))
    return jnp.concatenate([rows, jnp.broadcast_to(keys[:, None], (keys.shape[0], block))])


def body(sizes, x_blocks, col_slot, out_pos, out_count):
    n_row, n_col, n_depth = sizes
    n_rows, n_groups, block, _ = x_blocks.shape
    share = out_pos.shape[2] // n_depth
    slots = max(k for k in range(1, SLOTS + 1) if share % k == 0)
    n_chunks = 2 if n_groups % 2 == 0 else 1
    per = n_groups // n_chunks
    row, col, depth = lax.axis_index("row"), lax.axis_index("col"), lax.axis_index("depth")
    hops = lax.rem(col - row + n_col, n_col)
    kind = jnp.where(hops == 0, 0, 2 - hops % 2)
    info = jnp.stack([out_count[0, 0], row, depth, kind]).astype(jnp.int32)
    listed = lax.dynamic_slice_in_dim(out_pos[0, 0], depth * share, share)
    starts = listed // n_rows * (per * n_rows * block) + listed % n_rows * block
    pos = jnp.concatenate([listed, starts], 1).reshape(-1)
    evens, others = range(2, n_row, 2), range(1, n_depth)

    def hops_to(i, k, odd):
        ahead = (k - i // 2 * 2 + n_col) % n_col
        return lax.rem(ahead - (ahead + odd) % 2 + n_col, n_col)

    def next_col(value, step):
        return lax.ppermute(value, "col", [(i, (i + step) % n_col) for i in range(n_col)])

    def move(value, t, e, some=False):
        pairs = [
            (((i ^ t) * n_col + k) * n_depth + (j + e) % n_depth, (i * n_col + k) * n_depth + j)
            for i in range(n_row)
            for k in range(n_col)
            for j in range(n_depth)
            if not some or (k - i // 2 * 2) % n_col // 2
        ]
        return lax.ppermute(value, ("row", "col", "depth"), pairs)

    def choose(ring, t, odd):
        away = hops_to(row ^ t, col, odd)
        among = [k for k in range(1, n_col) if k % 2 == odd]
        value = ring[among[0]]
        for k in among[1:]:
            value = jnp.where(away == k, ring[k], value)
        return value

    def between_cores(pieces):
        for (t, e), value in list(pieces.items()):
            pieces[t + 1, e] = move(value, 1, 0)

    own = payload(x_blocks, col_slot)
    ring = {1: next_col(own, 1), n_col - 1: next_col(own, -1)}
    right = {(0, 0): own}
    for e in others:
        right[0, e] = move(own, 0, e)
    for t in evens:
        right[t, 0] = move(own, t, 0)
    for t in evens:
        for e in others:
            right[t, e] = move(right[0, e], t, 0)
    waited = [*ring.values(), *[right[at] for at in right if at != (0, 0)]]

    for k in range(2, n_col // 2 + 1):
        ring[k] = next_col(after(ring[k - 1], *ring.values()), 1)
    for k in range(n_col - 2, n_col // 2, -1):
        ring[k] = next_col(ring[k + 1], -1)
    first = {(0, 0): choose({**ring, 1: after(ring[1], *waited)}, 0, 1)}
    for e in others:
        first[0, e] = move(first[0, 0], 0, e)
    for t in evens:
        first[t, 0] = move(choose({**ring, 1: after(ring[1], *waited)}, t, 1), t, 0)
    waited = [*[first[at] for at in first if at != (0, 0)], *ring.values()]

    for t in evens:
        for e in others:
            first[t, e] = move(after(first[t, 0], *waited), 0, e)
    second = {}
    for t in range(0, n_row, 2):
        value = choose({**ring, 2: after(ring[2], *waited)}, t, 0)
        for e in range(n_depth):
            second[t, e] = move(value, t, e, True) if t or e else value
    for pieces in (right, first, second):
        between_cores(pieces)
    pieces = [(value, at, use) for use, part in enumerate((right, first, second)) for at, value in part.items()]
    plan = (n_row, n_depth, n_rows, share, slots, n_chunks, per)
    return products(plan, info, pos, pieces)[None, None]


def solution(mesh):
    sizes = tuple(mesh.shape[axis] for axis in ("row", "col", "depth"))
    in_specs = (
        P(("row", "col"), "depth", None, None),
        P(("row", "col"), "depth"),
        P("row", "col", None, None),
        P("row", "col"),
    )
    out_specs = P("row", "col", "depth", None, None)
    return jax.shard_map(
        functools.partial(body, sizes), mesh=mesh, in_specs=in_specs, out_specs=out_specs, check_vma=False
    )
```

```python
import functools

import jax
import jax.numpy as jnp
import numpy as np
from jax import lax
from jax.experimental import pallas as pl
from jax.experimental.pallas import tpu as pltpu
from jax.sharding import PartitionSpec as P

KEY_ROWS = 16
SLOTS = 48
TOGETHER = 8
BITS = 8


def bit_table():
    table = np.zeros(1 << BITS, np.int32)
    for mask in range(1 << BITS):
        there = [k for k in range(BITS) if mask >> k & 1]
        table[mask] = sum(k << 3 * i for i, k in enumerate(there)) + (len(there) << 3 * BITS)
    return table


def product_kernel(plan, places, slots, info, pos, table, *refs):
    n_row, n_depth, n_rows, n_groups, share = plan
    given, out, refs = refs[: len(places)], refs[len(places)], refs[len(places) + 1 :]
    panels, sums, tails, keys, bits, known, later, sems, tail_sems, known_sem = refs
    block = out.shape[-1]
    count, row, depth, kind = info[0], info[1], info[2], info[3]
    left = (kind == 0).astype(jnp.int32)
    step = pl.program_id(0)
    n_blocks = n_rows * n_groups
    none = n_depth * n_row * n_blocks
    possible = n_depth * n_groups
    parts = -(-possible // BITS)
    n_keys = tails.shape[3]
    room = share + TOGETHER
    lanes = bits.shape[1]
    rows_of_bits = bits.shape[0] // parts

    def block_of(side, at):
        return panels[side, pl.ds(pl.multiple_of(at * block, block), block), :]

    def known_of(part, slot):
        if isinstance(slot, int):
            return known[part * rows_of_bits + slot // lanes, slot % lanes]
        return known[part * rows_of_bits + lax.div(slot, lanes), lax.rem(slot, lanes)]

    def product(which, slot, j):
        lefts, rights = [], []
        for part in which:
            code = table[known_of(part, slot)]
            n = lax.shift_right_logical(code, 3 * BITS)
            for i in range(2):
                at = 2 * j + i
                which_one = part * BITS + (lax.shift_right_logical(code, 3 * at) & 7)
                start = table[(1 << BITS) + which_one]
                lefts.append(block_of(left, start + pos[2 * slot] * n_groups))
                rights.append(block_of(1, jnp.where(n > at, start + pos[2 * slot + 1] * n_groups, none)))
        return lax.dot_general(
            jnp.concatenate(lefts, 1),
            jnp.concatenate(rights, 1),
            (((1,), (1,)), ((), ())),
            preferred_element_type=jnp.float32,
        )

    @pl.when(step == 0)
    def _():
        def start(side, src, place, tail):
            r = row ^ place[0]
            if tail:
                src = src.at[pl.ds(n_blocks * block, n_keys)]
                pltpu.make_async_copy(src, tails.at[side, place[1], r], tail_sems.at[side]).start()
            else:
                src = src.at[pl.ds(0, n_blocks * block)]
                to = pl.ds((place[1] * n_row + r) * n_blocks * block, n_blocks * block)
                pltpu.make_async_copy(src, panels.at[side, to], sems.at[side]).start()

        def start_all(side, tail):
            for which in (1, 2) if side == 0 else (0,):

                @pl.when((kind == which) | (side == 1))
                def _():
                    for src, (place, use) in zip(given, places):
                        if use == which:
                            start(side, src, place, tail)

        start_all(1, True)
        start_all(0, True)
        start_all(1, False)
        panels[1, pl.ds(none * block, block), :] = jnp.zeros((block, block), panels.dtype)
        def read_keys(side):
            pltpu.make_async_copy(tails.at[side], tails.at[side], tail_sems.at[side]).wait()
            for e in range(n_depth):
                for r in range(n_row):
                    rows = tails[side, e, r].astype(jnp.float32)
                    for i in range(n_rows):
                        for g in range(n_groups):
                            at = i * n_groups + g
                            keys[side, r * n_rows + i, pl.ds(e * n_groups + g, 1), :] = rows[at : at + 1]

        read_keys(1)

        @pl.when(kind != 0)
        def _():
            read_keys(0)

        weight = jnp.left_shift(1, lax.broadcasted_iota(jnp.int32, (BITS, lanes), 0)).astype(jnp.float32)
        lane = lax.broadcasted_iota(jnp.int32, (1, lanes), 1)
        for part in range(parts):
            for at in range(rows_of_bits):
                found = jnp.zeros((1, lanes), jnp.float32)
                for slot in range(at * lanes, min(at * lanes + lanes, share)):
                    u, v = pos[2 * slot], pos[2 * slot + 1]
                    here = pl.ds(part * BITS, min(BITS, possible - part * BITS))
                    same = keys[left, u, here, :] == keys[1, v, here, :]
                    mine = jnp.sum(jnp.where(same, weight[: same.shape[0]], 0.0), 0, keepdims=True)
                    found = jnp.where(lane == slot - at * lanes, mine, found)
                bits[pl.ds(part * rows_of_bits + at, 1), :] = found.astype(jnp.int32)
        copy = pltpu.make_async_copy(bits, known, known_sem)
        copy.start()
        start_all(0, False)

        def clear(i, _):
            sums[i] = jnp.zeros((block, block), jnp.float32)
            return 0

        lax.fori_loop(0, share + 1, clear, 0)
        copy.wait()

        rounds = [(part, j) for part in range(parts) for j in range(1, BITS // 2)]

        totals = []
        for part in range(parts):
            total = jnp.int32(0)
            at = len(totals)
            for slot in range(share):
                later[at * room + total] = jnp.int32(slot)
                n = lax.shift_right_logical(table[known_of(part, slot)], 3 * BITS)
                total = total + (n > 2).astype(jnp.int32)
            totals.append(total)
            for j in range(2, BITS // 2):

                def more(k, total, at=at + j - 1, part=part, j=j):
                    slot = later[(at - 1) * room + k]
                    later[at * room + total] = slot
                    n = lax.shift_right_logical(table[known_of(part, slot)], 3 * BITS)
                    return total + (n > 2 * j).astype(jnp.int32)

                totals.append(lax.fori_loop(0, totals[-1], more, jnp.int32(0)))
        for i in range(len(rounds)):
            for k in range(TOGETHER):
                later[i * room + totals[i] + k] = jnp.int32(share)

        def wait_panel(side):
            whole = panels.at[side, pl.ds(0, none * block)]
            pltpu.make_async_copy(whole, whole, sems.at[side]).wait()

        wait_panel(1)

        @pl.when(kind != 0)
        def _():
            wait_panel(0)

        for i, (part, j) in enumerate(rounds):

            def some(k, _, i=i, part=part, j=j):
                which = [later[i * room + k * TOGETHER + m] for m in range(TOGETHER)]
                made = [product([part], slot, j) for slot in which]
                added = [sums[slot] + value for slot, value in zip(which, made)]
                for slot, value in zip(which, added):
                    sums[slot] = value
                return 0

            lax.fori_loop(0, lax.div(totals[i] + TOGETHER - 1, TOGETHER), some, 0)

    for k in range(slots):
        slot = step * slots + k
        value = product(range(parts), slot, 0) + sums[slot]
        out[k] = jnp.where(depth * share + slot < count, value, 0.0).astype(out.dtype)


def products(plan, info, pos, pieces):
    n_row, n_depth, n_rows, n_groups, share = plan
    slots = max(k for k in range(1, SLOTS + 1) if share % k == 0)
    rows, block = pieces[0][0].shape
    n_blocks = n_rows * n_groups
    total = n_depth * n_row * n_blocks
    possible = n_depth * n_groups
    parts = -(-possible // BITS)
    n_keys = rows - n_blocks * block
    places = [(place, use) for _, place, use in pieces]
    near = len(pieces) * rows * block * 2 <= 16 * 1024 * 1024
    args = [
        pltpu.with_memory_space_constraint(value, pltpu.VMEM if near and use == 2 else pltpu.HBM)
        for value, _, use in pieces
    ]
    starts = [k // n_groups * n_row * n_blocks + k % n_groups for k in range(possible)] + [0] * (parts * BITS - possible)
    table = jnp.asarray(np.concatenate([bit_table(), np.array(starts, np.int32)]))
    held = 2 * (total + 1) * block * block * 2 + 2 * slots * block * block * 2 + (share + 1) * block * block * 4
    return pl.pallas_call(
        functools.partial(product_kernel, plan, places, slots),
        grid=(share // slots,),
        in_specs=[pl.BlockSpec(memory_space=pltpu.SMEM)] * 3 + [pl.BlockSpec(memory_space=pl.ANY)] * len(args),
        out_specs=pl.BlockSpec((slots, block, block), lambda i: (i, 0, 0)),
        out_shape=jax.ShapeDtypeStruct((share, block, block), jnp.bfloat16),
        scratch_shapes=[
            pltpu.VMEM((2, (total + 1) * block, block), jnp.bfloat16),
            pltpu.VMEM((share + 1, block, block), jnp.float32),
            pltpu.VMEM((2, n_depth, n_row, n_keys, block), jnp.bfloat16),
            pltpu.VMEM((2, n_row * n_rows, parts * BITS, block), jnp.float32),
            pltpu.VMEM((parts * (share // block + 1), block), jnp.int32),
            pltpu.SMEM((parts * (share // block + 1), block), jnp.int32),
            pltpu.SMEM((parts * (BITS // 2 - 1) * (share + TOGETHER),), jnp.int32),
            pltpu.SemaphoreType.DMA((2,)),
            pltpu.SemaphoreType.DMA((2,)),
            pltpu.SemaphoreType.DMA,
        ],
        compiler_params=pltpu.CompilerParams(vmem_limit_bytes=held + 4 * 1024 * 1024),
        cost_estimate=pl.CostEstimate(
            flops=2 * share * possible * block**3,
            bytes_accessed=2 * total * block * block * 2 + share * block * block * 2,
            transcendentals=0,
        ),
    )(info, pos, table, *args)


def after(value, *others):
    return lax.optimization_barrier((value, *others))[0]


def payload(x_blocks, col_slot):
    block = x_blocks.shape[-1]
    keys = col_slot.reshape(-1).astype(x_blocks.dtype)
    keys = jnp.pad(keys, (0, -keys.shape[0] % KEY_ROWS))
    return jnp.concatenate([x_blocks.reshape(-1, block), jnp.broadcast_to(keys[:, None], (keys.shape[0], block))])


def body(sizes, x_blocks, col_slot, out_pos, out_count):
    n_row, n_col, n_depth = sizes
    n_rows, n_groups, block, _ = x_blocks.shape
    share = out_pos.shape[2] // n_depth
    row, col, depth = lax.axis_index("row"), lax.axis_index("col"), lax.axis_index("depth")
    hops = lax.rem(col - row + n_col, n_col)
    kind = jnp.where(hops == 0, 0, 2 - hops % 2)
    info = jnp.stack([out_count[0, 0], row, depth, kind]).astype(jnp.int32)
    listed = lax.dynamic_slice_in_dim(out_pos[0, 0], depth * share, share)
    pos = jnp.pad(listed.reshape(-1), (0, 2))
    evens, others = range(2, n_row, 2), range(1, n_depth)

    def hops_to(i, k, odd):
        ahead = (k - i // 2 * 2 + n_col) % n_col
        return lax.rem(ahead - (ahead + odd) % 2 + n_col, n_col)

    def next_col(value, step):
        return lax.ppermute(value, "col", [(i, (i + step) % n_col) for i in range(n_col)])

    def move(value, t, e, some=False):
        pairs = [
            (((i ^ t) * n_col + k) * n_depth + (j + e * (not some or needs_even(i, k))) % n_depth, (i * n_col + k) * n_depth + j)
            for i in range(n_row)
            for k in range(n_col)
            for j in range(n_depth)
        ]
        return lax.ppermute(value, ("row", "col", "depth"), pairs)

    def needs_even(i, k):
        return (k - i // 2 * 2) % n_col > 1

    def choose(ring, t, odd):
        away = hops_to(row ^ t, col, odd)
        among = [k for k in range(1, n_col) if k % 2 == odd]
        value = ring[among[0]]
        for k in among[1:]:
            value = jnp.where(away == k, ring[k], value)
        return value

    def between_cores(pieces):
        for (t, e), value in list(pieces.items()):
            pieces[t + 1, e] = move(value, 1, 0)

    own = payload(x_blocks, col_slot)
    ring = {1: next_col(own, 1), n_col - 1: next_col(own, -1)}
    right = {(0, 0): own}
    for e in others:
        right[0, e] = move(own, 0, e)
    for t in evens:
        right[t, 0] = move(own, t, 0)
    for t in evens:
        for e in others:
            right[t, e] = move(right[0, e], t, 0)
    waited = [*ring.values(), *[right[at] for at in right if at != (0, 0)]]

    for k in range(2, n_col // 2 + 1):
        ring[k] = next_col(after(ring[k - 1], *ring.values()), 1)
    for k in range(n_col - 2, n_col // 2, -1):
        ring[k] = next_col(ring[k + 1], -1)
    first = {(0, 0): choose({**ring, 1: after(ring[1], *waited)}, 0, 1)}
    for e in others:
        first[0, e] = move(first[0, 0], 0, e)
    for t in evens:
        first[t, 0] = move(choose({**ring, 1: after(ring[1], *waited)}, t, 1), t, 0)
    waited = [*[first[at] for at in first if at != (0, 0)], *ring.values()]

    for t in evens:
        for e in others:
            first[t, e] = move(after(first[t, 0], *waited), 0, e)
    second = {}
    for t in range(0, n_row, 2):
        value = choose({**ring, 2: after(ring[2], *waited)}, t, 0)
        for e in range(n_depth):
            second[t, e] = move(value, t, e, True) if t or e else value
    for pieces in (right, first, second):
        between_cores(pieces)
    pieces = [(value, at, use) for use, part in enumerate((right, first, second)) for at, value in part.items()]
    plan = (n_row, n_depth, n_rows, n_groups, share)
    return products(plan, info, pos, pieces)[None, None]


def solution(mesh):
    sizes = tuple(mesh.shape[axis] for axis in ("row", "col", "depth"))
    in_specs = (
        P(("row", "col"), "depth", None, None),
        P(("row", "col"), "depth"),
        P("row", "col", None, None),
        P("row", "col"),
    )
    out_specs = P("row", "col", "depth", None, None)
    return jax.shard_map(
        functools.partial(body, sizes), mesh=mesh, in_specs=in_specs, out_specs=out_specs, check_vma=False
    )
```

```python
import functools

import jax
import jax.numpy as jnp
import numpy as np
from jax import lax
from jax.experimental import pallas as pl
from jax.experimental.pallas import tpu as pltpu
from jax.sharding import PartitionSpec as P

KEY_ROWS = 16
SLOTS = 32
TOGETHER = 8
FIRST = 4
BITS = 8


def bit_table():
    table = np.zeros(1 << BITS, np.int32)
    for mask in range(1 << BITS):
        there = [k for k in range(BITS) if mask >> k & 1]
        table[mask] = sum(k << 3 * i for i, k in enumerate(there)) + (len(there) << 3 * BITS)
    return table


def product_kernel(plan, places, slots, info, pos, table, *refs):
    n_row, n_depth, n_rows, n_groups, share = plan
    given, out, refs = refs[: len(places)], refs[len(places)], refs[len(places) + 1 :]
    panels, sums, tails, keys, bits, known, later, sems, tail_sems, known_sem = refs
    block = out.shape[-1]
    count, row, depth, kind = info[0], info[1], info[2], info[3]
    left = (kind == 0).astype(jnp.int32)
    step = pl.program_id(0)
    n_blocks = n_rows * n_groups
    none = n_depth * n_row * n_blocks
    possible = n_depth * n_groups
    parts = -(-possible // BITS)
    n_keys = tails.shape[3]
    room = share + TOGETHER
    lanes = bits.shape[1]
    rows_of_bits = bits.shape[0] // parts

    def block_of(side, at):
        return panels[side, pl.ds(pl.multiple_of(at * block, block), block), :]

    def known_of(part, slot):
        if isinstance(slot, int):
            return known[part * rows_of_bits + slot // lanes, slot % lanes]
        return known[part * rows_of_bits + lax.div(slot, lanes), lax.rem(slot, lanes)]

    def product(which, slot, first, many):
        lefts, rights = [], []
        for part in which:
            code = table[known_of(part, slot)]
            n = lax.shift_right_logical(code, 3 * BITS)
            for at in range(first, first + many):
                which_one = part * BITS + (lax.shift_right_logical(code, 3 * at) & 7)
                start = table[(1 << BITS) + which_one]
                lefts.append(block_of(left, start + pos[2 * slot] * n_groups))
                rights.append(block_of(1, jnp.where(n > at, start + pos[2 * slot + 1] * n_groups, none)))
        return lax.dot_general(
            jnp.concatenate(lefts, 1),
            jnp.concatenate(rights, 1),
            (((1,), (1,)), ((), ())),
            preferred_element_type=jnp.float32,
        )

    @pl.when(step == 0)
    def _():
        def start(side, src, place, tail):
            r = row ^ place[0]
            if tail:
                src = src.at[pl.ds(n_blocks * block, n_keys)]
                pltpu.make_async_copy(src, tails.at[side, place[1], r], tail_sems.at[side]).start()
            else:
                src = src.at[pl.ds(0, n_blocks * block)]
                to = pl.ds((place[1] * n_row + r) * n_blocks * block, n_blocks * block)
                pltpu.make_async_copy(src, panels.at[side, to], sems.at[side]).start()

        def start_all(side, tail):
            for which in (1, 2) if side == 0 else (0,):

                @pl.when((kind == which) | (side == 1))
                def _():
                    for src, (place, use) in zip(given, places):
                        if use == which:
                            start(side, src, place, tail)

        start_all(1, True)
        start_all(0, True)
        start_all(1, False)
        panels[1, pl.ds(none * block, block), :] = jnp.zeros((block, block), panels.dtype)
        def read_keys(side):
            pltpu.make_async_copy(tails.at[side], tails.at[side], tail_sems.at[side]).wait()
            for e in range(n_depth):
                for r in range(n_row):
                    rows = tails[side, e, r].astype(jnp.float32)
                    for i in range(n_rows):
                        for g in range(n_groups):
                            at = i * n_groups + g
                            keys[side, r * n_rows + i, pl.ds(e * n_groups + g, 1), :] = rows[at : at + 1]

        read_keys(1)

        @pl.when(kind != 0)
        def _():
            read_keys(0)

        weight = jnp.left_shift(1, lax.broadcasted_iota(jnp.int32, (BITS, lanes), 0)).astype(jnp.float32)
        lane = lax.broadcasted_iota(jnp.int32, (1, lanes), 1)
        for part in range(parts):
            for at in range(rows_of_bits):
                found = jnp.zeros((1, lanes), jnp.float32)
                for slot in range(at * lanes, min(at * lanes + lanes, share)):
                    u, v = pos[2 * slot], pos[2 * slot + 1]
                    here = pl.ds(part * BITS, min(BITS, possible - part * BITS))
                    same = keys[left, u, here, :] == keys[1, v, here, :]
                    mine = jnp.sum(jnp.where(same, weight[: same.shape[0]], 0.0), 0, keepdims=True)
                    found = jnp.where(lane == slot - at * lanes, mine, found)
                bits[pl.ds(part * rows_of_bits + at, 1), :] = found.astype(jnp.int32)
        copy = pltpu.make_async_copy(bits, known, known_sem)
        copy.start()
        start_all(0, False)

        def clear(i, _):
            sums[i] = jnp.zeros((block, block), jnp.float32)
            return 0

        lax.fori_loop(0, share + 1, clear, 0)
        copy.wait()

        rounds = [(part, j) for part in range(parts) for j in range(FIRST // 2, BITS // 2)]

        totals = []
        for part in range(parts):
            total = jnp.int32(0)
            at = len(totals)
            for slot in range(share):
                later[at * room + total] = jnp.int32(slot)
                n = lax.shift_right_logical(table[known_of(part, slot)], 3 * BITS)
                total = total + (n > FIRST).astype(jnp.int32)
            totals.append(total)
            for j in range(FIRST // 2 + 1, BITS // 2):

                def more(k, total, at=at + j - FIRST // 2, part=part, j=j):
                    slot = later[(at - 1) * room + k]
                    later[at * room + total] = slot
                    n = lax.shift_right_logical(table[known_of(part, slot)], 3 * BITS)
                    return total + (n > 2 * j).astype(jnp.int32)

                totals.append(lax.fori_loop(0, totals[-1], more, jnp.int32(0)))
        for i in range(len(rounds)):
            for k in range(TOGETHER):
                later[i * room + totals[i] + k] = jnp.int32(share)

        def wait_panel(side):
            whole = panels.at[side, pl.ds(0, none * block)]
            pltpu.make_async_copy(whole, whole, sems.at[side]).wait()

        wait_panel(1)

        @pl.when(kind != 0)
        def _():
            wait_panel(0)

        for i, (part, j) in enumerate(rounds):

            def some(k, _, i=i, part=part, j=j):
                which = [later[i * room + k * TOGETHER + m] for m in range(TOGETHER)]
                made = [product([part], slot, 2 * j, 2) for slot in which]
                added = [sums[slot] + value for slot, value in zip(which, made)]
                for slot, value in zip(which, added):
                    sums[slot] = value
                return 0

            lax.fori_loop(0, lax.div(totals[i] + TOGETHER - 1, TOGETHER), some, 0)

    for k in range(slots):
        slot = step * slots + k
        value = product(range(parts), slot, 0, FIRST) + sums[slot]
        out[k] = jnp.where(depth * share + slot < count, value, 0.0).astype(out.dtype)


def products(plan, info, pos, pieces):
    n_row, n_depth, n_rows, n_groups, share = plan
    slots = max(k for k in range(1, SLOTS + 1) if share % k == 0)
    rows, block = pieces[0][0].shape
    n_blocks = n_rows * n_groups
    total = n_depth * n_row * n_blocks
    possible = n_depth * n_groups
    parts = -(-possible // BITS)
    n_keys = rows - n_blocks * block
    places = [(place, use) for _, place, use in pieces]
    near = len(pieces) * rows * block * 2 <= 16 * 1024 * 1024
    args = [
        pltpu.with_memory_space_constraint(value, pltpu.VMEM if near and use == 2 else pltpu.HBM)
        for value, place, use in pieces
    ]
    starts = [k // n_groups * n_row * n_blocks + k % n_groups for k in range(possible)] + [0] * (parts * BITS - possible)
    table = jnp.asarray(np.concatenate([bit_table(), np.array(starts, np.int32)]))
    held = 2 * (total + 1) * block * block * 2 + 2 * slots * block * block * 2 + (share + 1) * block * block * 4
    return pl.pallas_call(
        functools.partial(product_kernel, plan, places, slots),
        grid=(share // slots,),
        in_specs=[pl.BlockSpec(memory_space=pltpu.SMEM)] * 3 + [pl.BlockSpec(memory_space=pl.ANY)] * len(args),
        out_specs=pl.BlockSpec((slots, block, block), lambda i: (i, 0, 0)),
        out_shape=jax.ShapeDtypeStruct((share, block, block), jnp.bfloat16),
        scratch_shapes=[
            pltpu.VMEM((2, (total + 1) * block, block), jnp.bfloat16),
            pltpu.VMEM((share + 1, block, block), jnp.float32),
            pltpu.VMEM((2, n_depth, n_row, n_keys, block), jnp.bfloat16),
            pltpu.VMEM((2, n_row * n_rows, parts * BITS, block), jnp.float32),
            pltpu.VMEM((parts * (share // block + 1), block), jnp.int32),
            pltpu.SMEM((parts * (share // block + 1), block), jnp.int32),
            pltpu.SMEM((parts * (BITS // 2) * (share + TOGETHER),), jnp.int32),
            pltpu.SemaphoreType.DMA((2,)),
            pltpu.SemaphoreType.DMA((2,)),
            pltpu.SemaphoreType.DMA,
        ],
        compiler_params=pltpu.CompilerParams(vmem_limit_bytes=held + 3 * 512 * 1024),
        cost_estimate=pl.CostEstimate(
            flops=2 * share * possible * block**3,
            bytes_accessed=2 * total * block * block * 2 + share * block * block * 2,
            transcendentals=0,
        ),
    )(info, pos, table, *args)


def after(value, *others):
    return lax.optimization_barrier((value, *others))[0]


def payload(x_blocks, col_slot):
    block = x_blocks.shape[-1]
    keys = col_slot.reshape(-1).astype(x_blocks.dtype)
    keys = jnp.pad(keys, (0, -keys.shape[0] % KEY_ROWS))
    return jnp.concatenate([x_blocks.reshape(-1, block), jnp.broadcast_to(keys[:, None], (keys.shape[0], block))])


def body(sizes, x_blocks, col_slot, out_pos, out_count):
    n_row, n_col, n_depth = sizes
    n_rows, n_groups, block, _ = x_blocks.shape
    share = out_pos.shape[2] // n_depth
    row, col, depth = lax.axis_index("row"), lax.axis_index("col"), lax.axis_index("depth")
    hops = lax.rem(col - row + n_col, n_col)
    kind = jnp.where(hops == 0, 0, 2 - hops % 2)
    info = jnp.stack([out_count[0, 0], row, depth, kind]).astype(jnp.int32)
    listed = lax.dynamic_slice_in_dim(out_pos[0, 0], depth * share, share)
    pos = jnp.pad(listed.reshape(-1), (0, 2))
    evens, others = range(2, n_row, 2), range(1, n_depth)

    def hops_to(i, k, odd):
        ahead = (k - i // 2 * 2 + n_col) % n_col
        return lax.rem(ahead - (ahead + odd) % 2 + n_col, n_col)

    def next_col(value, step):
        return lax.ppermute(value, "col", [(i, (i + step) % n_col) for i in range(n_col)])

    def move(value, t, e, some=False):
        pairs = [
            (((i ^ t) * n_col + k) * n_depth + (j + e * (not some or needs_even(i, k))) % n_depth, (i * n_col + k) * n_depth + j)
            for i in range(n_row)
            for k in range(n_col)
            for j in range(n_depth)
        ]
        return lax.ppermute(value, ("row", "col", "depth"), pairs)

    def needs_even(i, k):
        return (k - i // 2 * 2) % n_col > 1

    def choose(ring, t, odd):
        away = hops_to(row ^ t, col, odd)
        among = [k for k in range(1, n_col) if k % 2 == odd]
        value = ring[among[0]]
        for k in among[1:]:
            value = jnp.where(away == k, ring[k], value)
        return value

    def between_cores(pieces):
        for (t, e), value in list(pieces.items()):
            pieces[t + 1, e] = move(value, 1, 0)

    own = payload(x_blocks, col_slot)
    ring = {1: next_col(own, 1), n_col - 1: next_col(own, -1)}
    right = {(0, 0): own}
    for e in others:
        right[0, e] = move(own, 0, e)
    for t in evens:
        right[t, 0] = move(own, t, 0)
    for t in evens:
        for e in others:
            right[t, e] = move(right[0, e], t, 0)
    waited = [*ring.values(), *[right[at] for at in right if at != (0, 0)]]

    for k in range(2, n_col // 2 + 1):
        ring[k] = next_col(after(ring[k - 1], *ring.values()), 1)
    for k in range(n_col - 2, n_col // 2, -1):
        ring[k] = next_col(ring[k + 1], -1)
    first = {(0, 0): choose({**ring, 1: after(ring[1], *waited)}, 0, 1)}
    for e in others:
        first[0, e] = move(first[0, 0], 0, e)
    for t in evens:
        first[t, 0] = move(choose({**ring, 1: after(ring[1], *waited, first[0, 0])}, t, 1), t, 0)
    waited = [*[first[at] for at in first if at != (0, 0)], *ring.values()]

    for t in evens:
        for e in others:
            first[t, e] = move(after(first[t, 0], *waited), 0, e)
    second = {}
    for t in range(0, n_row, 2):
        value = choose({**ring, 2: after(ring[2], *waited)}, t, 0)
        for e in range(n_depth):
            second[t, e] = move(value, t, e, True) if t or e else value
    for t in evens:
        for e in others:
            first[t, e] = after(first[t, e], *[second[at] for at in second if at != (0, 0)])
    for pieces in (right, first, second):
        between_cores(pieces)
    pieces = [(value, at, use) for use, part in enumerate((right, first, second)) for at, value in part.items()]
    plan = (n_row, n_depth, n_rows, n_groups, share)
    return products(plan, info, pos, pieces)[None, None]


def solution(mesh):
    sizes = tuple(mesh.shape[axis] for axis in ("row", "col", "depth"))
    in_specs = (
        P(("row", "col"), "depth", None, None),
        P(("row", "col"), "depth"),
        P("row", "col", None, None),
        P("row", "col"),
    )
    out_specs = P("row", "col", "depth", None, None)
    return jax.shard_map(
        functools.partial(body, sizes), mesh=mesh, in_specs=in_specs, out_specs=out_specs, check_vma=False
    )
```

```python
import functools

import jax
import jax.numpy as jnp
import numpy as np
from jax import lax
from jax.experimental import pallas as pl
from jax.experimental.pallas import tpu as pltpu
from jax.sharding import PartitionSpec as P

KEY_ROWS = 16
SLOTS = 32
TOGETHER = 8
FIRST = 4
BITS = 8


def bit_table():
    table = np.zeros(1 << BITS, np.int32)
    for mask in range(1 << BITS):
        there = [k for k in range(BITS) if mask >> k & 1]
        table[mask] = sum(k << 3 * i for i, k in enumerate(there)) + (len(there) << 3 * BITS)
    return table


def product_kernel(plan, places, slots, info, pos, table, *refs):
    n_row, n_depth, n_rows, n_groups, share = plan
    given, out, refs = refs[: len(places)], refs[len(places)], refs[len(places) + 1 :]
    panels, sums, tails, keys, bits, known, later, sems, tail_sems, known_sem = refs
    block = out.shape[-1]
    count, row, depth, kind = info[0], info[1], info[2], info[3]
    left = (kind == 0).astype(jnp.int32)
    step = pl.program_id(0)
    n_blocks = n_rows * n_groups
    none = n_depth * n_row * n_blocks
    possible = n_depth * n_groups
    parts = -(-possible // BITS)
    n_keys = tails.shape[3]
    room = share + TOGETHER
    lanes = bits.shape[1]
    rows_of_bits = bits.shape[0] // parts

    def block_of(side, at):
        return panels[side, pl.ds(pl.multiple_of(at * block, block), block), :]

    def known_of(part, slot):
        if isinstance(slot, int):
            return known[part * rows_of_bits + slot // lanes, slot % lanes]
        return known[part * rows_of_bits + lax.div(slot, lanes), lax.rem(slot, lanes)]

    def product(which, slot, first, many):
        lefts, rights = [], []
        for part in which:
            code = table[known_of(part, slot)]
            n = lax.shift_right_logical(code, 3 * BITS)
            for at in range(first, first + many):
                which_one = part * BITS + (lax.shift_right_logical(code, 3 * at) & 7)
                start = table[(1 << BITS) + which_one]
                lefts.append(block_of(left, start + pos[2 * slot] * n_groups))
                rights.append(block_of(1, jnp.where(n > at, start + pos[2 * slot + 1] * n_groups, none)))
        return lax.dot_general(
            jnp.concatenate(lefts, 1),
            jnp.concatenate(rights, 1),
            (((1,), (1,)), ((), ())),
            preferred_element_type=jnp.float32,
        )

    @pl.when(step == 0)
    def _():
        def start(side, src, place, tail):
            r = row ^ place[0]
            if tail:
                src = src.at[pl.ds(n_blocks * block, n_keys)]
                pltpu.make_async_copy(src, tails.at[side, place[1], r], tail_sems.at[side]).start()
            else:
                src = src.at[pl.ds(0, n_blocks * block)]
                to = pl.ds((place[1] * n_row + r) * n_blocks * block, n_blocks * block)
                pltpu.make_async_copy(src, panels.at[side, to], sems.at[side]).start()

        def start_all(side, tail):
            for which in (1, 2) if side == 0 else (0,):

                @pl.when((kind == which) | (side == 1))
                def _():
                    for src, (place, use) in zip(given, places):
                        if use == which:
                            start(side, src, place, tail)

        start_all(1, True)
        start_all(0, True)
        start_all(1, False)
        panels[1, pl.ds(none * block, block), :] = jnp.zeros((block, block), panels.dtype)
        def read_keys(side):
            pltpu.make_async_copy(tails.at[side], tails.at[side], tail_sems.at[side]).wait()
            for e in range(n_depth):
                for r in range(n_row):
                    rows = tails[side, e, r].astype(jnp.float32)
                    for i in range(n_rows):
                        for g in range(n_groups):
                            at = i * n_groups + g
                            keys[side, r * n_rows + i, pl.ds(e * n_groups + g, 1), :] = rows[at : at + 1]

        read_keys(1)

        @pl.when(kind != 0)
        def _():
            read_keys(0)

        weight = jnp.left_shift(1, lax.broadcasted_iota(jnp.int32, (BITS, lanes), 0)).astype(jnp.float32)
        lane = lax.broadcasted_iota(jnp.int32, (1, lanes), 1)
        for part in range(parts):
            for at in range(rows_of_bits):
                found = jnp.zeros((1, lanes), jnp.float32)
                for slot in range(at * lanes, min(at * lanes + lanes, share)):
                    u, v = pos[2 * slot], pos[2 * slot + 1]
                    here = pl.ds(part * BITS, min(BITS, possible - part * BITS))
                    same = keys[left, u, here, :] == keys[1, v, here, :]
                    mine = jnp.sum(jnp.where(same, weight[: same.shape[0]], 0.0), 0, keepdims=True)
                    found = jnp.where(lane == slot - at * lanes, mine, found)
                bits[pl.ds(part * rows_of_bits + at, 1), :] = found.astype(jnp.int32)
        copy = pltpu.make_async_copy(bits, known, known_sem)
        copy.start()
        start_all(0, False)

        def clear(i, _):
            sums[i] = jnp.zeros((block, block), jnp.float32)
            return 0

        lax.fori_loop(0, share + 1, clear, 0)
        copy.wait()

        rounds = [(part, j) for part in range(parts) for j in range(FIRST // 2, BITS // 2)]

        totals = []
        for part in range(parts):
            total = jnp.int32(0)
            at = len(totals)
            for slot in range(share):
                later[at * room + total] = jnp.int32(slot)
                n = lax.shift_right_logical(table[known_of(part, slot)], 3 * BITS)
                total = total + (n > FIRST).astype(jnp.int32)
            totals.append(total)
            for j in range(FIRST // 2 + 1, BITS // 2):

                def more(k, total, at=at + j - FIRST // 2, part=part, j=j):
                    slot = later[(at - 1) * room + k]
                    later[at * room + total] = slot
                    n = lax.shift_right_logical(table[known_of(part, slot)], 3 * BITS)
                    return total + (n > 2 * j).astype(jnp.int32)

                totals.append(lax.fori_loop(0, totals[-1], more, jnp.int32(0)))
        for i in range(len(rounds)):
            for k in range(TOGETHER):
                later[i * room + totals[i] + k] = jnp.int32(share)

        def wait_panel(side):
            whole = panels.at[side, pl.ds(0, none * block)]
            pltpu.make_async_copy(whole, whole, sems.at[side]).wait()

        wait_panel(1)

        @pl.when(kind != 0)
        def _():
            wait_panel(0)

        for i, (part, j) in enumerate(rounds):

            def some(k, _, i=i, part=part, j=j):
                which = [later[i * room + k * TOGETHER + m] for m in range(TOGETHER)]
                made = [product([part], slot, 2 * j, 2) for slot in which]
                added = [sums[slot] + value for slot, value in zip(which, made)]
                for slot, value in zip(which, added):
                    sums[slot] = value
                return 0

            lax.fori_loop(0, lax.div(totals[i] + TOGETHER - 1, TOGETHER), some, 0)

    for k in range(slots):
        slot = step * slots + k
        value = product(range(parts), slot, 0, FIRST) + sums[slot]
        out[k] = jnp.where(depth * share + slot < count, value, 0.0).astype(out.dtype)


def products(plan, info, pos, pieces):
    n_row, n_depth, n_rows, n_groups, share = plan
    slots = max(k for k in range(1, SLOTS + 1) if share % k == 0)
    rows, block = pieces[0][0].shape
    n_blocks = n_rows * n_groups
    total = n_depth * n_row * n_blocks
    possible = n_depth * n_groups
    parts = -(-possible // BITS)
    n_keys = rows - n_blocks * block
    places = [(place, use) for _, place, use in pieces]
    near = len(pieces) * rows * block * 2 <= 16 * 1024 * 1024
    args = [
        pltpu.with_memory_space_constraint(value, pltpu.VMEM if near and (use == 2 or use and place == (3, 1)) else pltpu.HBM)
        for value, place, use in pieces
    ]
    starts = [k // n_groups * n_row * n_blocks + k % n_groups for k in range(possible)] + [0] * (parts * BITS - possible)
    table = jnp.asarray(np.concatenate([bit_table(), np.array(starts, np.int32)]))
    held = 2 * (total + 1) * block * block * 2 + 2 * slots * block * block * 2 + (share + 1) * block * block * 4
    return pl.pallas_call(
        functools.partial(product_kernel, plan, places, slots),
        grid=(share // slots,),
        in_specs=[pl.BlockSpec(memory_space=pltpu.SMEM)] * 3 + [pl.BlockSpec(memory_space=pl.ANY)] * len(args),
        out_specs=pl.BlockSpec((slots, block, block), lambda i: (i, 0, 0)),
        out_shape=jax.ShapeDtypeStruct((share, block, block), jnp.bfloat16),
        scratch_shapes=[
            pltpu.VMEM((2, (total + 1) * block, block), jnp.bfloat16),
            pltpu.VMEM((share + 1, block, block), jnp.float32),
            pltpu.VMEM((2, n_depth, n_row, n_keys, block), jnp.bfloat16),
            pltpu.VMEM((2, n_row * n_rows, parts * BITS, block), jnp.float32),
            pltpu.VMEM((parts * (share // block + 1), block), jnp.int32),
            pltpu.SMEM((parts * (share // block + 1), block), jnp.int32),
            pltpu.SMEM((parts * (BITS // 2) * (share + TOGETHER),), jnp.int32),
            pltpu.SemaphoreType.DMA((2,)),
            pltpu.SemaphoreType.DMA((2,)),
            pltpu.SemaphoreType.DMA,
        ],
        compiler_params=pltpu.CompilerParams(vmem_limit_bytes=held + 3 * 512 * 1024),
        cost_estimate=pl.CostEstimate(
            flops=2 * share * possible * block**3,
            bytes_accessed=2 * total * block * block * 2 + share * block * block * 2,
            transcendentals=0,
        ),
    )(info, pos, table, *args)


def after(value, *others):
    return lax.optimization_barrier((value, *others))[0]


def payload(x_blocks, col_slot):
    block = x_blocks.shape[-1]
    keys = jnp.broadcast_to(col_slot[:, :, None], (*col_slot.shape, block)).reshape(-1, block)
    keys = jnp.pad(keys, ((0, -keys.shape[0] % KEY_ROWS), (0, 0)))
    return jnp.concatenate([x_blocks.reshape(-1, block), keys.astype(x_blocks.dtype)])


def body(sizes, x_blocks, col_slot, out_pos, out_count):
    n_row, n_col, n_depth = sizes
    n_rows, n_groups, block, _ = x_blocks.shape
    share = out_pos.shape[2] // n_depth
    row, col, depth = lax.axis_index("row"), lax.axis_index("col"), lax.axis_index("depth")
    hops = lax.rem(col - row + n_col, n_col)
    kind = jnp.where(hops == 0, 0, 2 - hops % 2)
    info = jnp.stack([out_count[0, 0], row, depth, kind]).astype(jnp.int32)
    listed = lax.dynamic_slice_in_dim(out_pos[0, 0], depth * share, share)
    pos = jnp.pad(listed.reshape(-1), (0, 2))
    evens, others = range(2, n_row, 2), range(1, n_depth)

    def hops_to(i, k, odd):
        ahead = (k - i // 2 * 2 + n_col) % n_col
        return lax.rem(ahead - (ahead + odd) % 2 + n_col, n_col)

    def next_col(value, step):
        return lax.ppermute(value, "col", [(i, (i + step) % n_col) for i in range(n_col)])

    def move(value, t, e, some=False):
        pairs = [
            (((i ^ t) * n_col + k) * n_depth + (j + e * (not some or needs_even(i, k))) % n_depth, (i * n_col + k) * n_depth + j)
            for i in range(n_row)
            for k in range(n_col)
            for j in range(n_depth)
        ]
        return lax.ppermute(value, ("row", "col", "depth"), pairs)

    def needs_even(i, k):
        return (k - i // 2 * 2) % n_col > 1

    def choose(ring, t, odd):
        away = hops_to(row ^ t, col, odd)
        among = [k for k in range(1, n_col) if k % 2 == odd]
        value = ring[among[0]]
        for k in among[1:]:
            value = jnp.where(away == k, ring[k], value)
        return value

    def between_cores(pieces):
        for (t, e), value in list(pieces.items()):
            pieces[t + 1, e] = move(value, 1, 0)

    own = payload(x_blocks, col_slot)
    ring = {1: next_col(own, 1), n_col - 1: next_col(own, -1)}
    right = {(0, 0): own}
    for e in others:
        right[0, e] = move(own, 0, e)
    for t in evens:
        right[t, 0] = move(own, t, 0)
    for t in evens:
        for e in others:
            right[t, e] = move(right[0, e], t, 0)
    waited = [*ring.values(), *[right[at] for at in right if at != (0, 0)]]

    for k in range(2, n_col // 2 + 1):
        ring[k] = next_col(after(ring[k - 1], *ring.values()), 1)
    for k in range(n_col - 2, n_col // 2, -1):
        ring[k] = next_col(ring[k + 1], -1)
    first = {(0, 0): choose({**ring, 1: after(ring[1], *waited)}, 0, 1)}
    for e in others:
        first[0, e] = move(first[0, 0], 0, e)
    for t in evens:
        first[t, 0] = move(choose({**ring, 1: after(ring[1], *waited, first[0, 0])}, t, 1), t, 0)
    waited = [*[first[at] for at in first if at != (0, 0)], *ring.values()]

    for t in evens:
        for e in others:
            first[t, e] = move(after(first[t, 0], *waited), 0, e)
    second = {}
    for t in range(0, n_row, 2):
        value = choose({**ring, 2: after(ring[2], *waited)}, t, 0)
        for e in range(n_depth):
            second[t, e] = move(value, t, e, True) if t or e else value
    for t in evens:
        for e in others:
            first[t, e] = after(first[t, e], *[second[at] for at in second if at != (0, 0)])
    for pieces in (right, first, second):
        between_cores(pieces)
    pieces = [(value, at, use) for use, part in enumerate((right, first, second)) for at, value in part.items()]
    pieces.sort(key=lambda piece: [1, 0, 2][piece[2]])
    plan = (n_row, n_depth, n_rows, n_groups, share)
    return products(plan, info, pos, pieces)[None, None]


def solution(mesh):
    sizes = tuple(mesh.shape[axis] for axis in ("row", "col", "depth"))
    in_specs = (
        P(("row", "col"), "depth", None, None),
        P(("row", "col"), "depth"),
        P("row", "col", None, None),
        P("row", "col"),
    )
    out_specs = P("row", "col", "depth", None, None)
    return jax.shard_map(
        functools.partial(body, sizes), mesh=mesh, in_specs=in_specs, out_specs=out_specs, check_vma=False
    )
```

```python
import functools

import jax
import jax.numpy as jnp
import numpy as np
from jax import lax
from jax.experimental import pallas as pl
from jax.experimental.pallas import tpu as pltpu
from jax.sharding import PartitionSpec as P

KEY_ROWS = 16
SLOTS = 48
TOGETHER = 8
FIRST = 4
BITS = 8


def bit_table():
    table = np.zeros(1 << BITS, np.int32)
    for mask in range(1 << BITS):
        there = [k for k in range(BITS) if mask >> k & 1]
        table[mask] = sum(k << 3 * i for i, k in enumerate(there)) + (len(there) << 3 * BITS)
    return table


def product_kernel(plan, places, slots, info, pos, table, *refs):
    n_row, n_depth, n_rows, n_groups, share = plan
    given, out, refs = refs[: len(places)], refs[len(places)], refs[len(places) + 1 :]
    panels, sums, tails, keys, bits, known, later, sems, tail_sems, known_sem = refs
    block = out.shape[-1]
    count, row, depth, kind = info[0], info[1], info[2], info[3]
    left = (kind == 0).astype(jnp.int32)
    step = pl.program_id(0)
    n_blocks = n_rows * n_groups
    none = n_depth * n_row * n_blocks
    possible = n_depth * n_groups
    parts = -(-possible // BITS)
    n_keys = tails.shape[3]
    room = share + TOGETHER
    lanes = bits.shape[1]
    rows_of_bits = bits.shape[0] // parts

    def block_of(side, at):
        return panels[side, pl.ds(pl.multiple_of(at * block, block), block), :]

    def known_of(part, slot):
        if isinstance(slot, int):
            return known[part * rows_of_bits + slot // lanes, slot % lanes]
        return known[part * rows_of_bits + lax.div(slot, lanes), lax.rem(slot, lanes)]

    def product(which, slot, first, many):
        lefts, rights = [], []
        for part in which:
            code = table[known_of(part, slot)]
            n = lax.shift_right_logical(code, 3 * BITS)
            for at in range(first, first + many):
                which_one = part * BITS + (lax.shift_right_logical(code, 3 * at) & 7)
                start = table[(1 << BITS) + which_one]
                lefts.append(block_of(left, start + pos[2 * slot] * n_groups))
                rights.append(block_of(1, jnp.where(n > at, start + pos[2 * slot + 1] * n_groups, none)))
        return lax.dot_general(
            jnp.concatenate(lefts, 1),
            jnp.concatenate(rights, 1),
            (((1,), (1,)), ((), ())),
            preferred_element_type=jnp.float32,
        )

    @pl.when(step == 0)
    def _():
        def start(side, src, place, tail):
            r = row ^ place[0]
            if tail:
                src = src.at[pl.ds(n_blocks * block, n_keys)]
                pltpu.make_async_copy(src, tails.at[side, place[1], r], tail_sems.at[side]).start()
            else:
                src = src.at[pl.ds(0, n_blocks * block)]
                to = pl.ds((place[1] * n_row + r) * n_blocks * block, n_blocks * block)
                pltpu.make_async_copy(src, panels.at[side, to], sems.at[side]).start()

        def start_all(side, tail):
            for which in (1, 2) if side == 0 else (0,):

                @pl.when((kind == which) | (side == 1))
                def _():
                    for src, (place, use) in zip(given, places):
                        if use == which:
                            start(side, src, place, tail)

        start_all(1, True)
        start_all(0, True)
        start_all(1, False)
        panels[1, pl.ds(none * block, block), :] = jnp.zeros((block, block), panels.dtype)
        def read_keys(side):
            pltpu.make_async_copy(tails.at[side], tails.at[side], tail_sems.at[side]).wait()
            for e in range(n_depth):
                for r in range(n_row):
                    rows = tails[side, e, r].astype(jnp.float32)
                    for i in range(n_rows):
                        for g in range(n_groups):
                            at = i * n_groups + g
                            keys[side, r * n_rows + i, pl.ds(e * n_groups + g, 1), :] = rows[at : at + 1]

        read_keys(1)

        @pl.when(kind != 0)
        def _():
            read_keys(0)

        weight = jnp.left_shift(1, lax.broadcasted_iota(jnp.int32, (BITS, lanes), 0)).astype(jnp.float32)
        lane = lax.broadcasted_iota(jnp.int32, (1, lanes), 1)
        for part in range(parts):
            for at in range(rows_of_bits):
                found = jnp.zeros((1, lanes), jnp.float32)
                for slot in range(at * lanes, min(at * lanes + lanes, share)):
                    u, v = pos[2 * slot], pos[2 * slot + 1]
                    here = pl.ds(part * BITS, min(BITS, possible - part * BITS))
                    same = keys[left, u, here, :] == keys[1, v, here, :]
                    mine = jnp.sum(jnp.where(same, weight[: same.shape[0]], 0.0), 0, keepdims=True)
                    found = jnp.where(lane == slot - at * lanes, mine, found)
                bits[pl.ds(part * rows_of_bits + at, 1), :] = found.astype(jnp.int32)
        copy = pltpu.make_async_copy(bits, known, known_sem)
        copy.start()
        start_all(0, False)

        def clear(i, _):
            sums[i] = jnp.zeros((block, block), jnp.float32)
            return 0

        lax.fori_loop(0, share + 1, clear, 0)
        copy.wait()

        rounds = [(part, j) for part in range(parts) for j in range(FIRST // 2, BITS // 2)]

        totals = []
        for part in range(parts):
            total = jnp.int32(0)
            at = len(totals)
            for slot in range(share):
                later[at * room + total] = jnp.int32(slot)
                n = lax.shift_right_logical(table[known_of(part, slot)], 3 * BITS)
                total = total + (n > FIRST).astype(jnp.int32)
            totals.append(total)
            for j in range(FIRST // 2 + 1, BITS // 2):

                def more(k, total, at=at + j - FIRST // 2, part=part, j=j):
                    slot = later[(at - 1) * room + k]
                    later[at * room + total] = slot
                    n = lax.shift_right_logical(table[known_of(part, slot)], 3 * BITS)
                    return total + (n > 2 * j).astype(jnp.int32)

                totals.append(lax.fori_loop(0, totals[-1], more, jnp.int32(0)))
        for i in range(len(rounds)):
            for k in range(TOGETHER):
                later[i * room + totals[i] + k] = jnp.int32(share)

        def wait_panel(side):
            whole = panels.at[side, pl.ds(0, none * block)]
            pltpu.make_async_copy(whole, whole, sems.at[side]).wait()

        wait_panel(1)

        @pl.when(kind != 0)
        def _():
            wait_panel(0)

        for i, (part, j) in enumerate(rounds):

            def some(k, _, i=i, part=part, j=j):
                which = [later[i * room + k * TOGETHER + m] for m in range(TOGETHER)]
                made = [product([part], slot, 2 * j, 2) for slot in which]
                added = [sums[slot] + value for slot, value in zip(which, made)]
                for slot, value in zip(which, added):
                    sums[slot] = value
                return 0

            lax.fori_loop(0, lax.div(totals[i] + TOGETHER - 1, TOGETHER), some, 0)

    for k in range(slots):
        slot = step * slots + k
        value = product(range(parts), slot, 0, FIRST) + sums[slot]
        out[k] = jnp.where(depth * share + slot < count, value, 0.0).astype(out.dtype)


def products(plan, info, pos, pieces):
    n_row, n_depth, n_rows, n_groups, share = plan
    slots = max(k for k in range(1, SLOTS + 1) if share % k == 0)
    rows, block = pieces[0][0].shape
    n_blocks = n_rows * n_groups
    total = n_depth * n_row * n_blocks
    possible = n_depth * n_groups
    parts = -(-possible // BITS)
    n_keys = rows - n_blocks * block
    places = [(place, use) for _, place, use in pieces]
    near = len(pieces) * rows * block * 2 <= 16 * 1024 * 1024
    args = [
        pltpu.with_memory_space_constraint(value, pltpu.VMEM if near and (use == 2 or use and place == (3, 1)) else pltpu.HBM)
        for value, place, use in pieces
    ]
    starts = [k // n_groups * n_row * n_blocks + k % n_groups for k in range(possible)] + [0] * (parts * BITS - possible)
    table = jnp.asarray(np.concatenate([bit_table(), np.array(starts, np.int32)]))
    held = 2 * (total + 1) * block * block * 2 + 2 * slots * block * block * 2 + (share + 1) * block * block * 4
    return pl.pallas_call(
        functools.partial(product_kernel, plan, places, slots),
        grid=(share // slots,),
        in_specs=[pl.BlockSpec(memory_space=pltpu.SMEM)] * 3 + [pl.BlockSpec(memory_space=pl.ANY)] * len(args),
        out_specs=pl.BlockSpec((slots, block, block), lambda i: (i, 0, 0)),
        out_shape=jax.ShapeDtypeStruct((share, block, block), jnp.bfloat16),
        scratch_shapes=[
            pltpu.VMEM((2, (total + 1) * block, block), jnp.bfloat16),
            pltpu.VMEM((share + 1, block, block), jnp.float32),
            pltpu.VMEM((2, n_depth, n_row, n_keys, block), jnp.bfloat16),
            pltpu.VMEM((2, n_row * n_rows, parts * BITS, block), jnp.float32),
            pltpu.VMEM((parts * (share // block + 1), block), jnp.int32),
            pltpu.SMEM((parts * (share // block + 1), block), jnp.int32),
            pltpu.SMEM((parts * (BITS // 2) * (share + TOGETHER),), jnp.int32),
            pltpu.SemaphoreType.DMA((2,)),
            pltpu.SemaphoreType.DMA((2,)),
            pltpu.SemaphoreType.DMA,
        ],
        compiler_params=pltpu.CompilerParams(vmem_limit_bytes=held + 3 * 512 * 1024),
        cost_estimate=pl.CostEstimate(
            flops=2 * share * possible * block**3,
            bytes_accessed=2 * total * block * block * 2 + share * block * block * 2,
            transcendentals=0,
        ),
    )(info, pos, table, *args)


def after(value, *others):
    return lax.optimization_barrier((value, *others))[0]


def payload(x_blocks, col_slot):
    block = x_blocks.shape[-1]
    keys = jnp.broadcast_to(col_slot[:, :, None], (*col_slot.shape, block)).reshape(-1, block)
    keys = jnp.pad(keys, ((0, -keys.shape[0] % KEY_ROWS), (0, 0)))
    return jnp.concatenate([x_blocks.reshape(-1, block), keys.astype(x_blocks.dtype)])


def body(sizes, x_blocks, col_slot, out_pos, out_count):
    n_row, n_col, n_depth = sizes
    n_rows, n_groups, block, _ = x_blocks.shape
    share = out_pos.shape[2] // n_depth
    row, col, depth = lax.axis_index("row"), lax.axis_index("col"), lax.axis_index("depth")
    hops = lax.rem(col - row + n_col, n_col)
    kind = jnp.where(hops == 0, 0, 2 - hops % 2)
    info = jnp.stack([out_count[0, 0], row, depth, kind]).astype(jnp.int32)
    listed = lax.dynamic_slice_in_dim(out_pos[0, 0], depth * share, share)
    pos = jnp.pad(listed.reshape(-1), (0, 2))
    evens, others = range(2, n_row, 2), range(1, n_depth)

    def hops_to(i, k, odd):
        ahead = (k - i // 2 * 2 + n_col) % n_col
        return lax.rem(ahead - (ahead + odd) % 2 + n_col, n_col)

    def next_col(value, step):
        return lax.ppermute(value, "col", [(i, (i + step) % n_col) for i in range(n_col)])

    def move(value, t, e, some=False):
        pairs = [
            (((i ^ t) * n_col + k) * n_depth + (j + e * (not some or needs_even(i, k))) % n_depth, (i * n_col + k) * n_depth + j)
            for i in range(n_row)
            for k in range(n_col)
            for j in range(n_depth)
        ]
        return lax.ppermute(value, ("row", "col", "depth"), pairs)

    def needs_even(i, k):
        return (k - i // 2 * 2) % n_col > 1

    def choose(ring, t, odd):
        away = hops_to(row ^ t, col, odd)
        among = [k for k in range(1, n_col) if k % 2 == odd]
        value = ring[among[0]]
        for k in among[1:]:
            value = jnp.where(away == k, ring[k], value)
        return value

    def between_cores(pieces):
        for (t, e), value in list(pieces.items()):
            pieces[t + 1, e] = move(value, 1, 0)

    own = payload(x_blocks, col_slot)
    ring = {1: next_col(own, 1), n_col - 1: next_col(own, -1)}
    right = {(0, 0): own}
    for e in others:
        right[0, e] = move(own, 0, e)
    for t in evens:
        right[t, 0] = move(own, t, 0)
    for t in evens:
        for e in others:
            right[t, e] = move(right[0, e], t, 0)
    waited = [*ring.values(), *[right[at] for at in right if at != (0, 0)]]

    for k in range(2, n_col // 2 + 1):
        ring[k] = next_col(after(ring[k - 1], *ring.values()), 1)
    for k in range(n_col - 2, n_col // 2, -1):
        ring[k] = next_col(ring[k + 1], -1)
    first = {(0, 0): choose({**ring, 1: after(ring[1], *waited)}, 0, 1)}
    for e in others:
        first[0, e] = move(first[0, 0], 0, e)
    for t in evens:
        first[t, 0] = move(choose({**ring, 1: after(ring[1], *waited, first[0, 0])}, t, 1), t, 0)
    waited = [*[first[at] for at in first if at != (0, 0)], *ring.values()]

    for t in evens:
        for e in others:
            first[t, e] = move(after(first[t, 0], *waited), 0, e)
    second = {}
    for t in range(0, n_row, 2):
        value = choose({**ring, 2: after(ring[2], *waited)}, t, 0)
        for e in range(n_depth):
            second[t, e] = move(value, t, e, True) if t or e else value
    for t in evens:
        for e in others:
            first[t, e] = after(first[t, e], *[second[at] for at in second if at != (0, 0)])
    for pieces in (right, first, second):
        between_cores(pieces)
    pieces = [(value, at, use) for use, part in enumerate((right, first, second)) for at, value in part.items()]
    pieces.sort(key=lambda piece: [1, 0, 2][piece[2]])
    plan = (n_row, n_depth, n_rows, n_groups, share)
    return products(plan, info, pos, pieces)[None, None]


def solution(mesh):
    sizes = tuple(mesh.shape[axis] for axis in ("row", "col", "depth"))
    in_specs = (
        P(("row", "col"), "depth", None, None),
        P(("row", "col"), "depth"),
        P("row", "col", None, None),
        P("row", "col"),
    )
    out_specs = P("row", "col", "depth", None, None)
    return jax.shard_map(
        functools.partial(body, sizes), mesh=mesh, in_specs=in_specs, out_specs=out_specs, check_vma=False
    )
```
